32 devices in a mesh: groups: 2 (over y), dp: 16 (over z, x, core).
Axes of the slice: x: 2, y: 2, z: 4, core: 2. Of those that a mesh axis runs over, the one named last changes fastest.
Arguments:
- hidden_acts: bfloat16 [32, 256, 16384], P(('groups', 'dp')), parts along dimension 0, as said below
- out_grads: bfloat16 [32, 256, 8192], P(('groups', 'dp')), parts along dimension 0, as said below
- proj_in: bfloat16 [64, 16384], P(None, 'dp'), may hold values from -0.046875 to 0.046875
- proj_out: bfloat16 [64, 8192], P(None, 'dp'), may hold values from -0.0625 to 0.0625
- lengths: int32 [32], P('groups'), parts along dimension 0, may hold values from 1 to 256, 2560 in all
- example_ids: int32 [32], P('groups'), parts along dimension 0, may hold values from 0 to 15, each once
Outputs:
- grad_store: float32 [32, 4096], P('groups', 'dp'), parts along dimension 0
- fisher_in: float32 [128, 64], P('groups'), parts along dimension 0
- fisher_out: float32 [128, 64], P('groups'), parts along dimension 0
The draws below stay inside these ranges and needn't reach their ends.
There are 2 independent parts, one for each index of `groups`. The reference program is written for one: setup_inputs(seed, part) draws one part's arguments, and reference() takes and returns one part's arrays. A program takes and returns all parts, laid end to end along the dimension named above; an argument that names none is the same for every part. Nothing has to cross between parts.
Inputs may be any that keep to these rules, and one draw needn't show every extreme that they name: `lengths`: the longest sequence has all 256 positions. `example_ids`: each store row is named by exactly one sequence. `hidden_acts`: activations drawn with feature and sequence scales. `out_grads`: gradients drawn with feature and sequence scales.
All inputs are finite; a program needn't handle non-finite values.
Results may differ from the reference program's by a relative error of at most 0.0005.
Values may be sent and summed in bfloat16 or wider, within the bound.
A program may use at most 64 MiB of HBM per device.

```python
import math
import jax
import jax.numpy as jnp
import numpy as np
from jax import lax

D = 8192
FFW = 16384
RANK = 64
SEQ = 256
SEQS = 16


def scaled_field(key, width):
    key_feat, key_seq, key_val = jax.random.split(key, 3)
    feature_scale = jnp.exp(jax.random.uniform(key_feat, (width,), jnp.float32) * math.log(10.0)) / 3.0
    seq_scale = jnp.exp(jax.random.uniform(key_seq, (SEQS, 1, 1), jnp.float32) * math.log(4.0)) / 2.0
    values = jax.random.normal(key_val, (SEQS, SEQ, width), jnp.float32)
    return (values * feature_scale[None, None, :] * seq_scale).astype(jnp.bfloat16)


def draw_hidden_acts(key, part):
    return scaled_field(jax.random.fold_in(key, 11), FFW)


def draw_out_grads(key, part):
    return scaled_field(jax.random.fold_in(key, 23), D)


def block_levels(own_key, dims, shards, low, largest):
    factor_of = 1.0
    for position, parts in shards:
        draws = jax.random.uniform(jax.random.fold_in(jax.random.fold_in(own_key, 6), position), (parts,), jnp.float32, low / len(shards), largest / len(shards))
        factor_of = factor_of * jnp.repeat(jnp.exp(draws), dims[position] // parts).reshape((-1,) + (1,) * (len(dims) - 1 - position))
    return factor_of


def profile(number_of, total, bound, lean):
    weights = [(1 << 20) // math.isqrt(standing ** lean) + 1 for standing in range(2, number_of + 1)]
    spare, given = total - bound - (number_of - 1), [1] * (number_of - 1)
    while spare > 0:
        movable = [i for i in range(number_of - 1) if given[i] < bound]
        whole, budget = sum([weights[i] for i in movable]), spare
        for i in movable:
            addition = min(bound - given[i], max(1, budget * weights[i] // whole), spare)
            given[i] = given[i] + addition
            spare = spare - addition
    return np.array([bound] + given)


def ragged_sizes(key, count, total, reach, skew):
    if count == 2:
        one = jax.random.randint(key, (), max(1, total - reach), min(reach, total - 1) + 1)
        return jnp.stack([one, total - one])
    sizes = jnp.asarray(profile(count, total, reach, skew), jnp.int32)
    couples = (count - 1) // 2
    donor, sink = sizes[1:1 + 2 * couples:2], sizes[2:2 + 2 * couples:2]
    slack = jnp.minimum(donor - 1, reach - sink)
    moved = jax.random.randint(jax.random.fold_in(key, 1), (couples,), 0, 1 << 20) % (slack + 1)
    sizes = sizes.at[1:1 + 2 * couples:2].set(donor - moved).at[2:2 + 2 * couples:2].set(sink + moved)
    return sizes[jax.random.permutation(jax.random.fold_in(key, 2), count)]


def scatter_about(stream_key, dims, scale, reach, shards=(), kind=jnp.bfloat16):
    loudness = block_levels(stream_key, dims, shards, -0.22, 0.18) if shards else 1.0
    array = jax.random.normal(stream_key, dims, jnp.float32) * scale * loudness
    return jnp.minimum(jnp.maximum(array, -reach), reach).astype(kind)


def setup_inputs(seed: int = 0, part: int = 0) -> dict:
    streams_of = jax.random.split(jax.random.key(seed), 7)
    part_splits = jax.random.split(jax.random.fold_in(streams_of[6], part), 7)
    return {
        "hidden_acts": draw_hidden_acts(jax.random.fold_in(jax.random.fold_in(streams_of[6], part), 71), part),
        "out_grads": draw_out_grads(jax.random.fold_in(jax.random.fold_in(streams_of[6], part), 71), part),
        "proj_in": scatter_about(streams_of[2], (RANK, FFW), FFW ** -0.5, 0.046875, ((1, 16),)),
        "proj_out": scatter_about(streams_of[3], (RANK, D), D ** -0.5, 0.0625, ((1, 16),)),
        "lengths": ragged_sizes(part_splits[4], SEQS, SEQS * SEQ * 5 // 8, SEQ, 0).astype(jnp.int32),
        "example_ids": jax.random.permutation(part_splits[5], SEQS).astype(jnp.int32),
    }


def reference(hidden_acts, out_grads, proj_in, proj_out, lengths, example_ids):
    live = (jnp.arange(SEQ, dtype=jnp.int32)[None, :] < lengths[:, None]).astype(jnp.float32)
    scale = 1.0 / math.sqrt(SEQ)

    def per_sequence(items):
        acts_one, grads_one, live_one = items
        in_side = jnp.dot(acts_one, proj_in.T, preferred_element_type=jnp.float32)
        out_side = jnp.dot(grads_one, proj_out.T, preferred_element_type=jnp.float32)
        in_live = in_side * live_one[:, None]
        out_live = out_side * live_one[:, None]
        example_grad = jnp.dot(out_live.T, in_side, precision=lax.Precision.HIGHEST) * scale
        factor_in = jnp.dot(in_live.T, in_side, precision=lax.Precision.HIGHEST)
        factor_out = jnp.dot(out_live.T, out_side, precision=lax.Precision.HIGHEST)
        return (example_grad, factor_in, factor_out)
    grads_all, factors_in, factors_out = lax.map(per_sequence, (hidden_acts, out_grads, live))
    count = jnp.sum(lengths).astype(jnp.float32)
    grad_store = jnp.zeros((SEQS, RANK * RANK), jnp.float32).at[example_ids].set(grads_all.reshape(SEQS, RANK * RANK))
    return (grad_store, lax.optimization_barrier(jnp.sum(factors_in, axis=0)) / count, lax.optimization_barrier(jnp.sum(factors_out, axis=0)) / count)
```

```python
import functools
import math

import jax
import jax.numpy as jnp
from jax import lax
from jax.experimental import pallas as pl
from jax.experimental.pallas import tpu as pltpu
from jax.sharding import PartitionSpec as P

KEYS = ((0, 0), (0, 1), (1, 0), (2, 0), (3, 0), (1, 1), (2, 1), (3, 1))
MESH = pl.DeviceIdType.MESH


def kernel(
    scale,
    acts_hbm, grads_hbm, pin_hbm, pout_hbm, lengths, ids,
    store_ref, fin_ref, fout_ref,
    acts, grads, gin, gout, acc_in, acc_out, slabs, terms, piece, totals,
    acts_sem, grads_sem, own_sem, send_sem, in_sem, out_sem,
    term_send, term_sem, tot_send, tot_sem,
):
    y = lax.axis_index("groups")
    me = lax.axis_index("dp")
    z, x, c = me // 4, (me // 2) % 2, me % 2
    devices = gin.shape[0]
    in_cols, out_cols = gin.shape[2], gout.shape[2]
    rank = fin_ref.shape[0]
    rows = rank // devices
    is_main = c == y

    def index(key, core):
        k, other = key
        return (z ^ k) * 4 + (x ^ other) * 2 + core

    order = [(KEYS[0], 0)]
    for i in range(1, len(KEYS)):
        order += [(KEYS[i], 0), (KEYS[i - 1], 1)]
    order.append((KEYS[-1], 1))
    pieces = [index(key, c ^ s) for key, s in order]

    own_in = pltpu.make_async_copy(pin_hbm, gin.at[me], own_sem.at[0])
    own_out = pltpu.make_async_copy(pout_hbm, gout.at[me], own_sem.at[1])
    own_in.start()
    own_out.start()
    barrier = pltpu.get_barrier_semaphore()
    for d in range(1, devices):
        pl.semaphore_signal(barrier, inc=1, device_id=(y, me ^ d), device_id_type=MESH)
    pl.semaphore_signal(barrier, inc=1, device_id=(1 - y, me), device_id_type=MESH)
    loads = []
    for n, p in enumerate(pieces):
        a = pltpu.make_async_copy(
            acts_hbm.at[:, pl.ds(pl.multiple_of(p * in_cols, in_cols), in_cols)],
            acts.at[n], acts_sem.at[n])
        b = pltpu.make_async_copy(
            grads_hbm.at[:, pl.ds(pl.multiple_of(p * out_cols, out_cols), out_cols)],
            grads.at[n], grads_sem.at[n])
        a.start()
        b.start()
        loads.append((a, b))
    own_in.wait()
    own_out.wait()
    pl.semaphore_wait(barrier, devices)

    sends = []

    def send(p, target, when=None):
        slot = len(sends)
        both = [
            pltpu.make_async_remote_copy(
                src_ref=buf.at[p], dst_ref=buf.at[p], send_sem=send_sem.at[j, slot],
                recv_sem=sem.at[p], device_id=target, device_id_type=MESH)
            for j, (buf, sem) in enumerate(((gin, in_sem), (gout, out_sem)))
        ]
        sends.append((both, when))
        if when is None:
            for copy in both:
                copy.start()
        else:
            @pl.when(when)
            def _():
                for copy in both:
                    copy.start()

    def arrived(p):
        for buf, sem in ((gin, in_sem), (gout, out_sem)):
            pltpu.make_async_copy(buf.at[p], buf.at[p], sem.at[p]).wait()

    across = (y, me ^ 2)
    sibling = (y, me ^ 1)
    opposite = (1 - y, me)

    def forward(key):
        p = index(key, c)
        k, other = key
        if other == 0:
            if k == 0:
                for d in (1, 3, 2):
                    send(p, (y, me ^ (4 * d)), is_main)
                send(p, across)
            else:
                send(p, opposite, is_main)
                send(p, across, None if k == 3 else is_main)
        elif k in (1, 2):
            send(p, opposite, is_main)
        send(p, sibling)

    acc_in[...] = jnp.zeros_like(acc_in)
    acc_out[...] = jnp.zeros_like(acc_out)
    for n, ((key, s), p) in enumerate(zip(order, pieces)):
        if n:
            arrived(p)
        if s == 0:
            forward(key)
        for copy in loads[n]:
            copy.wait()
        for acc, buf, g in ((acc_in, acts, gin), (acc_out, grads, gout)):
            acc[...] += lax.dot_general(
                buf[n], g[p], (((1,), (1,)), ((), ())),
                preferred_element_type=jnp.float32)

    both = jnp.concatenate([acc_in[...], acc_out[...]], axis=1)
    position = lax.broadcasted_iota(jnp.int32, both.shape, 0)
    live = jnp.where(position < lengths[me], both, 0.0)
    gram = lax.dot_general(
        live, both, (((0,), (0,)), ((), ())),
        precision=lax.Precision.HIGHEST, preferred_element_type=jnp.float32)
    for d in range(devices):
        slabs[d, 0:rows, :] = gram[d * rows:(d + 1) * rows, :]
        slabs[d, rows:2 * rows, :] = gram[rank + d * rows:rank + (d + 1) * rows, :]
    copies = []
    for d in range(1, devices):
        q = me ^ d
        copy = pltpu.make_async_remote_copy(
            src_ref=slabs.at[q], dst_ref=terms.at[me], send_sem=term_send.at[d],
            recv_sem=term_sem.at[me], device_id=(y, q), device_id_type=MESH)
        copy.start()
        copies.append(copy)
    terms[me] = slabs[me]
    count = lengths[0]
    for d in range(1, lengths.shape[0]):
        count = count + lengths[d]
    for d in range(1, devices):
        q = me ^ d
        pltpu.make_async_copy(slabs.at[q], terms.at[q], term_sem.at[q]).wait()
    total = terms[0]
    for d in range(1, devices):
        total = total + terms[d]
    total = total / jnp.full(total.shape, count.astype(jnp.float32))
    piece[...] = total
    for d in range(1, devices):
        copy = pltpu.make_async_remote_copy(
            src_ref=piece, dst_ref=totals.at[me], send_sem=tot_send.at[d],
            recv_sem=tot_sem.at[me], device_id=(y, me ^ d), device_id_type=MESH)
        copy.start()
        copies.append(copy)
    totals[me] = total
    row = lax.broadcasted_iota(jnp.int32, store_ref.shape, 0)
    store = jnp.zeros(store_ref.shape, jnp.float32)
    for d in range(devices):
        store = store + jnp.where(row == ids[d], terms[d, rows:2 * rows, :][None], 0.0)
    store_ref[...] = store * scale
    for d in range(1, devices):
        q = me ^ d
        pltpu.make_async_copy(piece, totals.at[q], tot_sem.at[q]).wait()
    for d in range(devices):
        fin_ref[d * rows:(d + 1) * rows, :] = totals[d, 0:rows, 0:rank]
        fout_ref[d * rows:(d + 1) * rows, :] = totals[d, rows:2 * rows, rank:2 * rank]
    for copy in copies:
        copy.wait_send()
    for pair, when in sends:
        if when is None:
            for copy in pair:
                copy.wait_send()
        else:
            @pl.when(when)
            def _():
                for copy in pair:
                    copy.wait_send()


def fused(hidden_acts, out_grads, proj_in, proj_out, lengths, example_ids):
    devices = lax.axis_size("dp")
    length, ffw = hidden_acts.shape[1:]
    width = out_grads.shape[2]
    rank, in_cols = proj_in.shape
    out_cols = proj_out.shape[1]
    rows = rank // devices
    f32, bf16 = jnp.float32, jnp.bfloat16
    dma = pltpu.SemaphoreType.DMA
    store, fin, fout = pl.pallas_call(
        functools.partial(kernel, 1.0 / math.sqrt(length)),
        out_shape=(
            jax.ShapeDtypeStruct((devices, rows, 2 * rank), f32),
            jax.ShapeDtypeStruct((rank, rank), f32),
            jax.ShapeDtypeStruct((rank, rank), f32),
        ),
        in_specs=[pl.BlockSpec(memory_space=pl.ANY)] * 4
        + [pl.BlockSpec(memory_space=pltpu.SMEM)] * 2,
        out_specs=[pl.BlockSpec(memory_space=pltpu.VMEM)] * 3,
        scratch_shapes=[
            pltpu.VMEM((devices, length, in_cols), bf16),
            pltpu.VMEM((devices, length, out_cols), bf16),
            pltpu.VMEM((devices, rank, in_cols), bf16),
            pltpu.VMEM((devices, rank, out_cols), bf16),
            pltpu.VMEM((length, rank), f32),
            pltpu.VMEM((length, rank), f32),
            pltpu.VMEM((devices, 2 * rows, 2 * rank), f32),
            pltpu.VMEM((devices, 2 * rows, 2 * rank), f32),
            pltpu.VMEM((2 * rows, 2 * rank), f32),
            pltpu.VMEM((devices, 2 * rows, 2 * rank), f32),
            dma((devices,)), dma((devices,)), dma((2,)), dma((2, 24)),
            dma((devices,)), dma((devices,)),
            dma((devices,)), dma((devices,)), dma((devices,)), dma((devices,)),
        ],
        compiler_params=pltpu.CompilerParams(
            collective_id=0, has_side_effects=True, vmem_limit_bytes=40 * 1024 * 1024),
        cost_estimate=pl.CostEstimate(
            flops=2 * length * rank * (ffw + width),
            bytes_accessed=2 * length * (ffw + width), transcendentals=0),
    )(hidden_acts.reshape(length, ffw), out_grads.reshape(length, width),
      proj_in, proj_out, lengths, example_ids)
    return store[:, :, :rank].reshape(devices, rows * rank), fin, fout


def local(hidden_acts, out_grads, proj_in, proj_out, lengths, example_ids):
    devices = lax.axis_size("dp")
    seq_block = lax.axis_index("dp")
    seq_count = hidden_acts.shape[0]
    local_len = hidden_acts.shape[1]
    rows = seq_count * local_len
    rank = proj_in.shape[0]
    in_cols = proj_in.shape[1]
    out_cols = proj_out.shape[1]
    total_seqs = example_ids.shape[0]
    flat_acts = hidden_acts.reshape(rows, in_cols * devices)
    flat_grads = out_grads.reshape(rows, out_cols * devices)
    joined = jnp.concatenate([proj_in, proj_out], axis=1)[None]
    gathered = lax.all_gather(joined, "dp", axis=0, tiled=True)
    in_side = jnp.einsum(
        "tnc,nrc->tr",
        flat_acts.reshape(rows, devices, in_cols),
        gathered[:, :, :in_cols],
        preferred_element_type=jnp.float32,
    )
    out_side = jnp.einsum(
        "tnc,nrc->tr",
        flat_grads.reshape(rows, devices, out_cols),
        gathered[:, :, in_cols:],
        preferred_element_type=jnp.float32,
    )
    first_seq = seq_block * seq_count
    my_lengths = lax.dynamic_slice_in_dim(lengths, first_seq, seq_count, 0)
    positions = jnp.arange(local_len, dtype=jnp.int32)
    live_mask = (positions[None, :] < my_lengths[:, None]).astype(jnp.float32)
    in_side = in_side.reshape(seq_count, local_len, rank)
    out_side = out_side.reshape(seq_count, local_len, rank)
    in_live = in_side * live_mask[:, :, None]
    out_live = out_side * live_mask[:, :, None]
    high = lax.Precision.HIGHEST
    example_terms = jnp.einsum("sci,scj->sij", out_live, in_side, precision=high).reshape(
        seq_count, rank * rank
    )
    factor_in = jnp.einsum("sci,scj->ij", in_live, in_side, precision=high)
    factor_out = jnp.einsum("sci,scj->ij", out_live, out_side, precision=high)
    count = jnp.sum(lengths).astype(jnp.float32)
    scale = 1.0 / math.sqrt(local_len)
    piece_width = rank * rank // devices
    outgoing = example_terms.reshape(seq_count, devices, piece_width)
    received = lax.all_to_all(outgoing, "dp", split_axis=1, concat_axis=0, tiled=True)
    received = received.reshape(total_seqs, piece_width)
    store_rows = jnp.arange(total_seqs, dtype=jnp.int32)
    routing_table = (store_rows[:, None] == example_ids[None, :]).astype(jnp.float32)
    store_part = jnp.dot(routing_table, received, precision=high)
    summed_in, summed_out = lax.psum((factor_in, factor_out), "dp")
    return (store_part * scale, summed_in / count, summed_out / count)


def solution(mesh):
    in_specs = (
        P(("groups", "dp"), None, None),
        P(("groups", "dp"), None, None),
        P(None, "dp"),
        P(None, "dp"),
        P("groups"),
        P("groups"),
    )
    out_specs = (P("groups", "dp"), P("groups", None), P("groups", None))
    fits = mesh.shape["groups"] == 2 and mesh.shape["dp"] == 16

    def body(*args):
        return (fused if fits and args[0].shape[0] == 1 else local)(*args)

    return jax.shard_map(body, mesh=mesh, in_specs=in_specs, out_specs=out_specs, check_vma=False)
```

```python
import functools
import math

import jax
import jax.numpy as jnp
from jax import lax
from jax.experimental import pallas as pl
from jax.experimental.pallas import tpu as pltpu
from jax.sharding import PartitionSpec as P

KEYS = ((0, 0), (1, 0), (0, 1), (2, 0), (1, 1), (3, 0), (2, 1), (3, 1))
LAG = 4
CHUNKS = 3
MESH = pl.DeviceIdType.MESH


def kernel(
    scale,
    acts_hbm, grads_hbm, pin_hbm, pout_hbm, lengths, ids,
    store_ref, fin_ref, fout_ref,
    acts, grads, gin, gout, acc_in, acc_out, slabs, terms, examples, grads_in, piece, totals,
    acts_sem, grads_sem, own_sem, send_sem, in_sem,
    term_send, term_sem, example_send, example_sem, tot_send, tot_sem,
):
    y = lax.axis_index("groups")
    me = lax.axis_index("dp")
    z, x, c = me // 4, (me // 2) % 2, me % 2
    devices = gin.shape[0]
    in_cols, out_cols = gin.shape[2], gout.shape[2]
    rank = fin_ref.shape[0]
    rows = rank // devices
    is_main = c == y

    inner = jnp.logical_or(z == 1, z == 2)
    planes = (z, z ^ 1, z ^ jnp.where(inner, 3, 2), z ^ jnp.where(inner, 2, 3))

    def index(key, core):
        step, other = key
        return planes[step] * 4 + (x ^ other) * 2 + core

    order = []
    for i in range(len(KEYS) + LAG):
        if i < len(KEYS):
            order.append((KEYS[i], 0))
        if i >= LAG:
            order.append((KEYS[i - LAG], 1))
    pieces = [index(key, c ^ s) for key, s in order]

    own_in = pltpu.make_async_copy(pin_hbm, gin.at[me], own_sem.at[0])
    own_out = pltpu.make_async_copy(pout_hbm, gout.at[me], own_sem.at[1])
    own_in.start()
    own_out.start()
    barrier = pltpu.get_barrier_semaphore()
    for d in (1, 2):
        pl.semaphore_signal(barrier, inc=1, device_id=(y, me ^ d), device_id_type=MESH)

    @pl.when(z < 3)
    def _():
        pl.semaphore_signal(barrier, inc=1, device_id=(y, me + 4), device_id_type=MESH)

    @pl.when(z > 0)
    def _():
        pl.semaphore_signal(barrier, inc=1, device_id=(y, me - 4), device_id_type=MESH)

    pl.semaphore_signal(barrier, inc=1, device_id=(1 - y, me), device_id_type=MESH)
    loads = []
    for n, p in enumerate(pieces):
        a = pltpu.make_async_copy(
            acts_hbm.at[:, pl.ds(pl.multiple_of(p * in_cols, in_cols), in_cols)],
            acts.at[n], acts_sem.at[n])
        b = pltpu.make_async_copy(
            grads_hbm.at[:, pl.ds(pl.multiple_of(p * out_cols, out_cols), out_cols)],
            grads.at[n], grads_sem.at[n])
        a.start()
        b.start()
        loads.append((a, b))
    own_in.wait()
    own_out.wait()
    pl.semaphore_wait(barrier, 3 + (z < 3).astype(jnp.int32) + (z > 0).astype(jnp.int32))

    sends = []

    def chunk(j, p):
        if j == 2:
            return gout.at[p]
        half = rank // 2
        return gin.at[p, pl.ds(j * half, half), :]

    def send(j, p, target, when=None):
        slot = len(sends)
        copy = pltpu.make_async_remote_copy(
            src_ref=chunk(j, p), dst_ref=chunk(j, p), send_sem=send_sem.at[slot],
            recv_sem=in_sem.at[j, p], device_id=target, device_id_type=MESH)
        sends.append((copy, when))
        if when is None:
            copy.start()
        else:
            pl.when(when)(copy.start)

    def arrived(j, p):
        pltpu.make_async_copy(chunk(j, p), chunk(j, p), in_sem.at[j, p]).wait()

    across = (y, me ^ 2)
    sibling = (y, me ^ 1)
    opposite = (1 - y, me)

    def forward(j, key):
        p = index(key, c)
        step, other = key
        if other == 0:
            line = jnp.logical_or(is_main, j == 2)
            plane = planes[step]
            up = jnp.logical_and(plane <= z, z < 3)
            down = jnp.logical_and(plane >= z, z > 0)
            if step == 0:
                send(j, p, (y, jnp.where(up, me + 4, me)), jnp.logical_and(line, up))
                send(j, p, (y, jnp.where(down, me - 4, me)), jnp.logical_and(line, down))
                send(j, p, across)
            else:
                send(j, p, (y, jnp.where(up, me + 4, jnp.where(down, me - 4, me))),
                     jnp.logical_and(line, jnp.logical_or(up, down)))
                send(j, p, across, is_main)
                if j < 2:
                    send(j, p, opposite, is_main)
        elif step:
            send(j, p, opposite, is_main)
        send(j, p, sibling)

    acc_in[...] = jnp.zeros_like(acc_in)
    acc_out[...] = jnp.zeros_like(acc_out)
    for n, ((key, s), p) in enumerate(zip(order, pieces)):
        for j in range(CHUNKS):
            if n:
                arrived(j, p)
            if s == 0:
                forward(j, key)
        for copy in loads[n]:
            copy.wait()
        for acc, buf, g in ((acc_in, acts, gin), (acc_out, grads, gout)):
            acc[...] += lax.dot_general(
                buf[n], g[p], (((1,), (1,)), ((), ())),
                preferred_element_type=jnp.float32)

    both = jnp.concatenate([acc_in[...], acc_out[...]], axis=1)
    position = lax.broadcasted_iota(jnp.int32, both.shape, 0)
    live = jnp.where(position < lengths[me], both, 0.0)
    gram = lax.dot_general(
        live, both, (((0,), (0,)), ((), ())),
        precision=lax.Precision.HIGHEST, preferred_element_type=jnp.float32)
    lane = lax.broadcasted_iota(jnp.int32, (rank, 2 * rank), 1)
    factors = jnp.where(lane < rank, gram[:rank, :], gram[rank:, :])
    copies = []

    def scatter(slabs, terms, sends, arrivals):
        for d in reversed(range(1, devices)):
            q = me ^ d
            copy = pltpu.make_async_remote_copy(
                src_ref=slabs.at[q], dst_ref=terms.at[me], send_sem=sends.at[d],
                recv_sem=arrivals.at[me], device_id=(y, q), device_id_type=MESH)
            copy.start()
            copies.append(copy)
        terms[me] = slabs[me]

    def collect(terms, arrivals):
        for d in range(1, devices):
            q = me ^ d
            pltpu.make_async_copy(terms.at[q], terms.at[q], arrivals.at[q]).wait()

    for d in range(devices):
        slabs[d] = factors[d * rows:(d + 1) * rows, :]
    scatter(slabs, terms, term_send, term_sem)
    for d in range(devices):
        examples[d] = gram[rank + d * rows:rank + (d + 1) * rows, :]
    scatter(examples, grads_in, example_send, example_sem)
    count = lengths[0]
    for d in range(1, lengths.shape[0]):
        count = count + lengths[d]
    collect(terms, term_sem)
    total = jnp.sum(terms[...], axis=0)
    total = total / jnp.full(total.shape, count.astype(jnp.float32))
    piece[...] = total
    for d in reversed(range(1, devices)):
        copy = pltpu.make_async_remote_copy(
            src_ref=piece, dst_ref=totals.at[me], send_sem=tot_send.at[d],
            recv_sem=tot_sem.at[me], device_id=(y, me ^ d), device_id_type=MESH)
        copy.start()
        copies.append(copy)
    totals[me] = total
    collect(grads_in, example_sem)
    row = lax.broadcasted_iota(jnp.int32, store_ref.shape, 0)
    store = jnp.zeros(store_ref.shape, jnp.float32)
    for d in range(devices):
        store = store + jnp.where(row == ids[d], grads_in[d][None], 0.0)
    store_ref[...] = store * scale
    collect(totals, tot_sem)
    for d in range(devices):
        fin_ref[d * rows:(d + 1) * rows, :] = totals[d, :, 0:rank]
        fout_ref[d * rows:(d + 1) * rows, :] = totals[d, :, rank:2 * rank]
    for copy in copies:
        copy.wait_send()
    for copy, when in sends:
        if when is None:
            copy.wait_send()
        else:
            pl.when(when)(copy.wait_send)


def place(store_in, fin_in, fout_in, store_ref, fin_ref, fout_ref):
    rank = fin_in.shape[0]
    for q in range(store_in.shape[1]):
        store_ref[:, q * rank:(q + 1) * rank] = store_in[:, q, 0:rank]
    fin_ref[...] = fin_in[...]
    fout_ref[...] = fout_in[...]


def fused(hidden_acts, out_grads, proj_in, proj_out, lengths, example_ids):
    devices = lax.axis_size("dp")
    length, ffw = hidden_acts.shape[1:]
    width = out_grads.shape[2]
    rank, in_cols = proj_in.shape
    out_cols = proj_out.shape[1]
    rows = rank // devices
    f32, bf16 = jnp.float32, jnp.bfloat16
    dma = pltpu.SemaphoreType.DMA
    store, fin, fout = pl.pallas_call(
        functools.partial(kernel, 1.0 / math.sqrt(length)),
        out_shape=(
            jax.ShapeDtypeStruct((devices, rows, 2 * rank), f32),
            jax.ShapeDtypeStruct((rank, rank), f32),
            jax.ShapeDtypeStruct((rank, rank), f32),
        ),
        in_specs=[pl.BlockSpec(memory_space=pl.ANY)] * 4
        + [pl.BlockSpec(memory_space=pltpu.SMEM)] * 2,
        out_specs=[pl.BlockSpec(memory_space=pltpu.VMEM)] * 3,
        scratch_shapes=[
            pltpu.VMEM((devices, length, in_cols), bf16),
            pltpu.VMEM((devices, length, out_cols), bf16),
            pltpu.VMEM((devices, rank, in_cols), bf16),
            pltpu.VMEM((devices, rank, out_cols), bf16),
            pltpu.VMEM((length, rank), f32),
            pltpu.VMEM((length, rank), f32),
            pltpu.VMEM((devices, rows, 2 * rank), f32),
            pltpu.VMEM((devices, rows, 2 * rank), f32),
            pltpu.VMEM((devices, rows, 2 * rank), f32),
            pltpu.VMEM((devices, rows, 2 * rank), f32),
            pltpu.VMEM((rows, 2 * rank), f32),
            pltpu.VMEM((devices, rows, 2 * rank), f32),
            dma((devices,)), dma((devices,)), dma((2,)), dma((96,)),
            dma((CHUNKS, devices)),
            dma((devices,)), dma((devices,)), dma((devices,)),
            dma((devices,)), dma((devices,)), dma((devices,)),
        ],
        compiler_params=pltpu.CompilerParams(
            collective_id=0, has_side_effects=True, vmem_limit_bytes=58 * 1024 * 1024),
        cost_estimate=pl.CostEstimate(
            flops=2 * length * rank * (ffw + width),
            bytes_accessed=2 * length * (ffw + width), transcendentals=0),
    )(hidden_acts.reshape(length, ffw), out_grads.reshape(length, width),
      proj_in, proj_out, lengths, example_ids)
    return pl.pallas_call(
        place,
        out_shape=(
            jax.ShapeDtypeStruct((devices, rows * rank), f32),
            jax.ShapeDtypeStruct((rank, rank), f32),
            jax.ShapeDtypeStruct((rank, rank), f32),
        ),
        in_specs=[pl.BlockSpec(memory_space=pltpu.VMEM)] * 3,
        out_specs=[pl.BlockSpec(memory_space=pltpu.VMEM)] * 3,
    )(store, fin, fout)


def local(hidden_acts, out_grads, proj_in, proj_out, lengths, example_ids):
    devices = lax.axis_size("dp")
    seq_block = lax.axis_index("dp")
    seq_count = hidden_acts.shape[0]
    local_len = hidden_acts.shape[1]
    rows = seq_count * local_len
    rank = proj_in.shape[0]
    in_cols = proj_in.shape[1]
    out_cols = proj_out.shape[1]
    total_seqs = example_ids.shape[0]
    flat_acts = hidden_acts.reshape(rows, in_cols * devices)
    flat_grads = out_grads.reshape(rows, out_cols * devices)
    joined = jnp.concatenate([proj_in, proj_out], axis=1)[None]
    gathered = lax.all_gather(joined, "dp", axis=0, tiled=True)
    in_side = jnp.einsum(
        "tnc,nrc->tr",
        flat_acts.reshape(rows, devices, in_cols),
        gathered[:, :, :in_cols],
        preferred_element_type=jnp.float32,
    )
    out_side = jnp.einsum(
        "tnc,nrc->tr",
        flat_grads.reshape(rows, devices, out_cols),
        gathered[:, :, in_cols:],
        preferred_element_type=jnp.float32,
    )
    first_seq = seq_block * seq_count
    my_lengths = lax.dynamic_slice_in_dim(lengths, first_seq, seq_count, 0)
    positions = jnp.arange(local_len, dtype=jnp.int32)
    live_mask = (positions[None, :] < my_lengths[:, None]).astype(jnp.float32)
    in_side = in_side.reshape(seq_count, local_len, rank)
    out_side = out_side.reshape(seq_count, local_len, rank)
    in_live = in_side * live_mask[:, :, None]
    out_live = out_side * live_mask[:, :, None]
    high = lax.Precision.HIGHEST
    example_terms = jnp.einsum("sci,scj->sij", out_live, in_side, precision=high).reshape(
        seq_count, rank * rank
    )
    factor_in = jnp.einsum("sci,scj->ij", in_live, in_side, precision=high)
    factor_out = jnp.einsum("sci,scj->ij", out_live, out_side, precision=high)
    count = jnp.sum(lengths).astype(jnp.float32)
    scale = 1.0 / math.sqrt(local_len)
    piece_width = rank * rank // devices
    outgoing = example_terms.reshape(seq_count, devices, piece_width)
    received = lax.all_to_all(outgoing, "dp", split_axis=1, concat_axis=0, tiled=True)
    received = received.reshape(total_seqs, piece_width)
    store_rows = jnp.arange(total_seqs, dtype=jnp.int32)
    routing_table = (store_rows[:, None] == example_ids[None, :]).astype(jnp.float32)
    store_part = jnp.dot(routing_table, received, precision=high)
    summed_in, summed_out = lax.psum((factor_in, factor_out), "dp")
    return (store_part * scale, summed_in / count, summed_out / count)


def solution(mesh):
    in_specs = (
        P(("groups", "dp"), None, None),
        P(("groups", "dp"), None, None),
        P(None, "dp"),
        P(None, "dp"),
        P("groups"),
        P("groups"),
    )
    out_specs = (P("groups", "dp"), P("groups", None), P("groups", None))
    fits = mesh.shape["groups"] == 2 and mesh.shape["dp"] == 16

    def body(*args):
        return (fused if fits and args[0].shape[0] == 1 else local)(*args)

    return jax.shard_map(body, mesh=mesh, in_specs=in_specs, out_specs=out_specs, check_vma=False)
```
